32 devices in a mesh: frame: 16 (over z, y, x), mp: 2 (over core).
Axes of the slice: x: 2, y: 2, z: 4, core: 2. Of those that a mesh axis runs over, the one named last changes fastest.
Arguments:
- stream: bfloat16 [16, 1024, 1280], P('frame'), may hold values from -6 to 6
- spatial_qkv: bfloat16 [16, 1024, 3, 1280], P('frame', None, None, 'mp'), may hold values from -30 to 30
- spatial_out_w: bfloat16 [1280, 1280], P('mp'), may hold values from -0.625 to 0.625
- temporal_gain: bfloat16 [1280], replicated, may hold values from 0.5 to 1.5
- temporal_qkv_w: bfloat16 [3, 1280, 1280], P(None, None, 'mp'), may hold values from -0.15625 to 0.15625
- temporal_out_w: bfloat16 [1280, 1280], P('mp'), may hold values from -0.625 to 0.625
- decoder_gain: bfloat16 [1280], replicated, may hold values from 0.5 to 1.5
- decoder_kv_w: bfloat16 [2, 1280, 512], P(None, None, 'mp'), may hold values from -0.15625 to 0.15625
- vertex_queries: bfloat16 [778, 512], P(None, 'mp'), may hold values from -6 to 6
- crop_counts: int32 [16], replicated, may hold values from 0 to 3, as said below
- crop_tiles: int32 [16, 3], replicated, may hold values from 0 to 7
- crop_owner: int32 [16, 3], replicated, may hold values from 0 to 15, as said below
Outputs:
- vertex_features: bfloat16 [64, 512, 778], P('frame', 'mp')
- final_stream: bfloat16 [16, 1024, 1280], P('frame', None, 'mp')
The draws below stay inside these ranges and needn't reach their ends.
Inputs may be any that keep to these rules, and one draw needn't show every extreme that they name: `crop_counts`: some frame has exactly 3 crops. `crop_owner`: the slots of one frame name different owners; no owner is named by more than 4 live slots, and some owner by exactly 4.
All inputs are finite; a program needn't handle non-finite values.
Results may differ from the reference program's by a relative error of at most 0.028.
Values may be sent and summed in bfloat16 or wider, within the bound.
A program may use at most 128 MiB of HBM per device.

```python
import jax
import jax.numpy as jnp
from jax import lax

D = 1280
HEADS = 16
HD = 80
FRAMES = 16
P_SIZE = 1024
TILE = 128
MAXC = 3
RCAP = 4
DEC = 512
DEC_HEADS = 8
DEC_HD = 64
V = 778
SLOTS = 64
N_MP = 2


def draw_spatial_qkv(key, part):
    normal_draw = jnp.clip(jax.random.normal(key, (FRAMES, P_SIZE, 3, D), jnp.float32), -6.0, 6.0)
    normal_draw = normal_draw.at[:, :, 0].multiply(2.0)
    return normal_draw.astype(jnp.bfloat16)


def crop_plan(key):
    order = jax.random.permutation(jax.random.fold_in(key, 7), FRAMES)
    position = jnp.argsort(order).astype(jnp.int32)
    start_counts = jax.random.randint(jax.random.fold_in(key, 8), (FRAMES,), 0, 3)
    counts = jnp.where(position < RCAP, jnp.maximum(start_counts, 1), start_counts)
    counts = jnp.where(position == RCAP, MAXC, counts)
    shifts = jax.random.randint(jax.random.fold_in(key, 9), (FRAMES // RCAP,), 0, RCAP)
    owner_block = position // RCAP
    slot_ids = jnp.arange(MAXC, dtype=jnp.int32)[None, :]
    owners = RCAP * owner_block[:, None] + (slot_ids + shifts[owner_block][:, None]) % RCAP
    return (counts.astype(jnp.int32), owners.astype(jnp.int32))


def draw_crop_counts(key, part):
    return crop_plan(key)[0]


def draw_crop_owner(key, part):
    return crop_plan(key)[1]


def place_ends(values, key, smallest, largest):
    dims = values.shape
    index_at = [jax.random.randint(jax.random.fold_in(key, axis), (), 0, dims[axis]) for axis in range(len(dims))]
    values = values.at[tuple(index_at)].set(smallest)
    longest = dims.index(max(dims))
    index_at[longest] = (index_at[longest] + 1) % dims[longest]
    return values.at[tuple(index_at)].set(largest)


def steps_of(stream_key, shape, cuts, smallest, largest):
    factor_of = 1.0
    for dim, blocks in cuts:
        steps = jax.random.uniform(jax.random.fold_in(jax.random.fold_in(stream_key, 6), dim), (blocks,), jnp.float32, smallest / len(cuts), largest / len(cuts))
        factor_of = factor_of * jnp.repeat(jnp.exp(steps), shape[dim] // blocks).reshape((-1,) + (1,) * (len(shape) - 1 - dim))
    return factor_of


def bell_draw(stream_key, dims, deviation, limit, shards=(), held_as=jnp.bfloat16):
    level = steps_of(stream_key, dims, shards, -0.22, 0.18) if shards else 1.0
    result = jax.random.normal(stream_key, dims, jnp.float32) * deviation * level
    return jnp.minimum(jnp.maximum(result, -limit), limit).astype(held_as)


def setup_inputs(seed: int = 0) -> dict:
    key_of = jax.random.split(jax.random.key(seed), 13)
    stream = bell_draw(key_of[0], (FRAMES, P_SIZE, D), 1.0, 6.0, ((0, 16),))
    spatial_qkv = draw_spatial_qkv(jax.random.fold_in(key_of[12], 71), 0)
    spatial_out_w = bell_draw(key_of[2], (D, D), (D // 16) ** -0.5, 0.625, ((0, 2),))
    temporal_gain = jnp.clip(1.0 + 0.1 * jax.random.normal(key_of[3], (D,), jnp.float32), 0.5, 1.5).astype(jnp.bfloat16)
    temporal_qkv_w = bell_draw(key_of[4], (3, D, D), D ** -0.5, 0.15625, ((2, 2),))
    temporal_out_w = bell_draw(key_of[5], (D, D), (D // 16) ** -0.5, 0.625, ((0, 2),))
    decoder_gain = jnp.clip(1.0 + 0.1 * jax.random.normal(key_of[6], (D,), jnp.float32), 0.5, 1.5).astype(jnp.bfloat16)
    decoder_kv_w = bell_draw(key_of[7], (2, D, DEC), D ** -0.5, 0.15625, ((2, 2),))
    vertex_queries = bell_draw(key_of[8], (V, DEC), 1.0, 6.0, ((1, 2),))
    crop_counts = draw_crop_counts(jax.random.fold_in(key_of[12], 71), 0)
    crop_tiles = place_ends(jax.random.randint(key_of[10], (FRAMES, MAXC), 0, P_SIZE // TILE), jax.random.fold_in(key_of[10], 1), 0, (P_SIZE // TILE) - 1).astype(jnp.int32)
    crop_owner = draw_crop_owner(jax.random.fold_in(key_of[12], 71), 0)
    return dict(stream=stream, spatial_qkv=spatial_qkv, spatial_out_w=spatial_out_w, temporal_gain=temporal_gain, temporal_qkv_w=temporal_qkv_w, temporal_out_w=temporal_out_w, decoder_gain=decoder_gain, decoder_kv_w=decoder_kv_w, vertex_queries=vertex_queries, crop_counts=crop_counts, crop_tiles=crop_tiles, crop_owner=crop_owner)


def upcast(values):
    return lax.optimization_barrier(values).astype(jnp.float32)

def layer_norm(values, gain_row):
    row_mean = lax.optimization_barrier(jnp.mean(values, axis=-1, keepdims=True))
    centred = values - row_mean
    spread = lax.optimization_barrier(jnp.mean(centred * centred, axis=-1, keepdims=True))
    return (centred * lax.rsqrt(spread + 1e-06) * gain_row.astype(jnp.float32)).astype(jnp.bfloat16)

def soft_weights(scores):
    row_top = lax.optimization_barrier(jnp.max(scores, axis=-1, keepdims=True))
    raised = jnp.exp(scores - row_top)
    return (raised / lax.optimization_barrier(jnp.sum(raised, axis=-1, keepdims=True))).astype(jnp.bfloat16)

def crop_slots(crop_counts, crop_owner):
    frames_all, most = crop_owner.shape
    live_slots = (jnp.arange(most, dtype=jnp.int32)[None, :] < crop_counts[:, None]).reshape(-1)
    owner_flat = crop_owner.reshape(-1)
    owner_hits = ((owner_flat[:, None] == jnp.arange(frames_all, dtype=jnp.int32)[None, :]) & live_slots[:, None]).astype(jnp.int32)
    before = jnp.cumsum(owner_hits, axis=0) - owner_hits
    slot_rank = lax.optimization_barrier(jnp.sum(before * owner_hits, axis=1))
    return (live_slots, owner_flat * RCAP + slot_rank)

def grouped_sum(heads, weight):
    group_cols = D // N_MP
    flat_heads = heads.reshape(-1, D)
    running = jnp.zeros((flat_heads.shape[0], D), jnp.float32)
    for group in range(N_MP):
        lower = group * group_cols
        partial_sum = jnp.dot(flat_heads[:, lower:lower + group_cols], weight[lower:lower + group_cols], preferred_element_type=jnp.float32)
        running = running + upcast(partial_sum.astype(jnp.bfloat16))
    return running.reshape(heads.shape)

def reference(stream, spatial_qkv, spatial_out_w, temporal_gain, temporal_qkv_w, temporal_out_w, decoder_gain, decoder_kv_w, vertex_queries, crop_counts, crop_tiles, crop_owner):
    score_scale = HD ** (-0.5)

    def spatial_frame(qkv_block):
        qkv_parts = qkv_block.astype(jnp.float32).reshape(P_SIZE, 3, HEADS, HD)
        scores = jnp.einsum('qhd,khd->hqk', qkv_parts[:, 0], qkv_parts[:, 1]) * score_scale
        weights = soft_weights(scores)
        spatial_heads = jnp.einsum('hqk,khd->qhd', upcast(weights), qkv_parts[:, 2])
        return spatial_heads.reshape(P_SIZE, D).astype(jnp.bfloat16)
    spatial_heads = lax.map(spatial_frame, spatial_qkv)
    middle = (stream.astype(jnp.float32) + grouped_sum(spatial_heads, spatial_out_w)).astype(jnp.bfloat16)
    normed = layer_norm(middle.astype(jnp.float32), temporal_gain)
    flat_normed = normed.reshape(FRAMES * P_SIZE, D)
    projected = [upcast(jnp.dot(flat_normed, temporal_qkv_w[which], preferred_element_type=jnp.float32).astype(jnp.bfloat16)).reshape(FRAMES, P_SIZE, HEADS, HD) for which in range(3)]
    scores = jnp.einsum('fphd,gphd->phfg', projected[0], projected[1]) * score_scale
    weights = soft_weights(scores)
    temporal_heads = jnp.einsum('phfg,gphd->fphd', upcast(weights), projected[2]).reshape(FRAMES, P_SIZE, D).astype(jnp.bfloat16)
    final_stream = (middle.astype(jnp.float32) + grouped_sum(temporal_heads, temporal_out_w)).astype(jnp.bfloat16)
    tile_view = final_stream.reshape(FRAMES, P_SIZE // TILE, TILE, D)
    crop_rows = jnp.take_along_axis(tile_view, crop_tiles.astype(jnp.int32)[:, :, None, None], axis=1)
    crop_norm = layer_norm(crop_rows.astype(jnp.float32), decoder_gain).reshape(FRAMES * MAXC * TILE, D)
    crop_keys = jnp.dot(crop_norm, decoder_kv_w[0], preferred_element_type=jnp.float32).astype(jnp.bfloat16).reshape(FRAMES * MAXC, TILE, DEC)
    crop_values = jnp.dot(crop_norm, decoder_kv_w[1], preferred_element_type=jnp.float32).astype(jnp.bfloat16).reshape(FRAMES * MAXC, TILE, DEC)
    live_slots, slot_index = crop_slots(crop_counts, crop_owner)
    placing = ((slot_index[:, None] == jnp.arange(SLOTS, dtype=jnp.int32)[None, :]) & live_slots[:, None]).astype(jnp.float32)
    slot_keys = jnp.einsum('ks,ktc->stc', placing, upcast(crop_keys), precision=lax.Precision.HIGHEST).astype(jnp.bfloat16)
    slot_values = jnp.einsum('ks,ktc->stc', placing, upcast(crop_values), precision=lax.Precision.HIGHEST).astype(jnp.bfloat16)
    vertex_wide = vertex_queries.astype(jnp.float32).reshape(V, DEC_HEADS, DEC_HD)

    def decode(slot_pair):
        pair_keys = upcast(slot_pair[0]).reshape(TILE, DEC_HEADS, DEC_HD)
        pair_values = upcast(slot_pair[1]).reshape(TILE, DEC_HEADS, DEC_HD)
        vertex_scores = jnp.einsum('vhd,thd->hvt', vertex_wide, pair_keys) * DEC_HD ** (-0.5)
        vertex_weights = soft_weights(vertex_scores)
        decoded = jnp.einsum('hvt,thd->hdv', upcast(vertex_weights), pair_values)
        return decoded.reshape(DEC, V).astype(jnp.bfloat16)
    vertex_features = lax.map(decode, (slot_keys, slot_values))
    return (vertex_features, final_stream)
```

```python
import functools

import jax
import jax.numpy as jnp
from jax import lax
from jax.experimental import pallas as pl
from jax.experimental.pallas import tpu as pltpu
from jax.sharding import PartitionSpec as P

HD = 80
TILE = 128
MAXC = 3
RCAP = 4
DEC_HD = 64
V = 778
ROWS = 256
PATCHES = 16
LOG2E = 1.4426950408889634
MIB = 1 << 20


def layer_norm(values, gain_row):
    row_mean = jnp.mean(values, axis=-1, keepdims=True)
    centred = values - row_mean
    spread = jnp.mean(centred * centred, axis=-1, keepdims=True)
    return (centred * lax.rsqrt(spread + 1e-06) * gain_row.astype(jnp.float32)).astype(jnp.bfloat16)


def soft_weights(scores):
    row_top = jnp.max(scores, axis=-1, keepdims=True)
    raised = jnp.exp(scores - row_top)
    return (raised / jnp.sum(raised, axis=-1, keepdims=True)).astype(jnp.bfloat16)


def crop_slots(crop_counts, crop_owner):
    frames_all, most = crop_owner.shape
    live_slots = (jnp.arange(most, dtype=jnp.int32)[None, :] < crop_counts[:, None]).reshape(-1)
    owner_flat = crop_owner.reshape(-1)
    owner_hits = (
        (owner_flat[:, None] == jnp.arange(frames_all, dtype=jnp.int32)[None, :])
        & live_slots[:, None]
    ).astype(jnp.int32)
    before = jnp.cumsum(owner_hits, axis=0) - owner_hits
    slot_rank = jnp.sum(before * owner_hits, axis=1)
    return (live_slots, owner_flat * RCAP + slot_rank)


def on_device_any(
    stream,
    spatial_qkv,
    spatial_out_w,
    temporal_gain,
    temporal_qkv_w,
    temporal_out_w,
    decoder_gain,
    decoder_kv_w,
    vertex_queries,
    crop_counts,
    crop_tiles,
    crop_owner,
):
    patches = stream.shape[1]
    model_width = stream.shape[2]
    local_cols = spatial_qkv.shape[3]
    heads_here = local_cols // HD
    score_scale = HD ** (-0.5)
    spatial_query = spatial_qkv[0, :, 0].reshape(patches, heads_here, HD)
    spatial_key = spatial_qkv[0, :, 1].reshape(patches, heads_here, HD)
    spatial_value = spatial_qkv[0, :, 2].reshape(patches, heads_here, HD)
    scores = (
        jnp.einsum("qhd,khd->hqk", spatial_query, spatial_key, preferred_element_type=jnp.float32)
        * score_scale
    )
    weights = soft_weights(scores)
    spatial_heads = (
        jnp.einsum("hqk,khd->qhd", weights, spatial_value, preferred_element_type=jnp.float32)
        .astype(jnp.bfloat16)
        .reshape(patches, local_cols)
    )
    spatial_part = jnp.dot(spatial_heads, spatial_out_w, preferred_element_type=jnp.float32)
    spatial_total = lax.psum(spatial_part.astype(jnp.bfloat16), "mp").astype(jnp.float32)
    middle = (stream[0].astype(jnp.float32) + spatial_total).astype(jnp.bfloat16)
    normed = layer_norm(middle.astype(jnp.float32), temporal_gain)
    projected = jnp.stack(
        [
            jnp.dot(normed, temporal_qkv_w[which], preferred_element_type=jnp.float32).astype(
                jnp.bfloat16
            )
            for which in range(3)
        ],
        axis=1,
    )[None]
    gathered = lax.all_to_all(projected, "frame", split_axis=1, concat_axis=0, tiled=True)
    frames_all = gathered.shape[0]
    patch_rows = gathered.shape[1]
    temporal_query = gathered[:, :, 0].reshape(frames_all, patch_rows, heads_here, HD)
    temporal_key = gathered[:, :, 1].reshape(frames_all, patch_rows, heads_here, HD)
    temporal_value = gathered[:, :, 2].reshape(frames_all, patch_rows, heads_here, HD)
    frame_scores = (
        jnp.einsum(
            "fphd,gphd->phfg", temporal_query, temporal_key, preferred_element_type=jnp.float32
        )
        * score_scale
    )
    frame_weights = soft_weights(frame_scores)
    mixed_heads = (
        jnp.einsum(
            "phfg,gphd->fphd", frame_weights, temporal_value, preferred_element_type=jnp.float32
        )
        .astype(jnp.bfloat16)
        .reshape(frames_all, patch_rows, local_cols)
    )
    frame_heads = lax.all_to_all(mixed_heads, "frame", split_axis=0, concat_axis=1, tiled=True)
    temporal_part = jnp.dot(frame_heads[0], temporal_out_w, preferred_element_type=jnp.float32)
    temporal_total = lax.psum(temporal_part.astype(jnp.bfloat16), "mp").astype(jnp.float32)
    final_stream = (middle.astype(jnp.float32) + temporal_total).astype(jnp.bfloat16)
    out_cols = model_width // lax.axis_size("mp")
    stream_part = lax.dynamic_slice_in_dim(
        final_stream, lax.axis_index("mp") * out_cols, out_cols, 1
    )[None]
    frame_id = lax.axis_index("frame")
    my_tiles = lax.dynamic_index_in_dim(crop_tiles, frame_id, 0, keepdims=False)
    tile_view = final_stream.reshape(patches // TILE, TILE, model_width)
    crop_rows = jnp.take(tile_view, my_tiles, axis=0)
    crop_norm = layer_norm(crop_rows.astype(jnp.float32), decoder_gain).reshape(
        MAXC * TILE, model_width
    )
    return decode(
        crop_norm, decoder_kv_w, vertex_queries, crop_counts, crop_owner
    ), stream_part


def head_window(head):
    first = head * HD // 128 * 128
    last = -(-(head + 1) * HD // 128) * 128
    return first, last - first, head * HD - first


def head_attention(query, key_of, value_of, out_ref, row_slice, heads_here, keep):
    factor = HD ** (-0.5) * LOG2E
    done = {}
    for head in range(heads_here):
        first, width, start = head_window(head)
        lane = lax.broadcasted_iota(jnp.int32, (1, width), 1)
        inside = (lane >= start) & (lane < start + HD)
        q_here = query[:, first : first + width]
        q_here = jnp.where(inside, q_here, jnp.zeros_like(q_here))
        scores = lax.dot_general(
            q_here,
            key_of(first, width),
            (((1,), (1,)), ((), ())),
            preferred_element_type=jnp.float32,
        )
        if keep is not None:
            scores = jnp.where(keep, scores, -jnp.inf)
        top = jnp.max(scores, axis=-1, keepdims=True)
        raised = jnp.exp2(scores * factor - top * factor).astype(jnp.bfloat16)
        v_here = value_of(first, width)
        v_here = jnp.where(inside, v_here, jnp.ones_like(v_here))
        both = jnp.dot(raised, v_here, preferred_element_type=jnp.float32)
        at = 0 if start else width - 1
        found = (both / both[:, at : at + 1]).astype(jnp.bfloat16)
        for tile in range(width // 128):
            column = first + tile * 128
            part = found[:, tile * 128 : tile * 128 + 128]
            if column in done:
                part = jnp.where(inside[:, tile * 128 : tile * 128 + 128], part, done[column])
            done[column] = part
    for column, part in done.items():
        out_ref[row_slice, column : column + 128] = part


def spatial_kernel(q_ref, k_ref, v_ref, w_ref, mine_ref, other_ref, heads_ref):
    here = lax.axis_index("mp")
    cols = q_ref.shape[1]
    head_attention(
        q_ref[...],
        lambda first, width: k_ref[:, first : first + width],
        lambda first, width: v_ref[:, first : first + width],
        heads_ref,
        slice(None),
        cols // HD,
        None,
    )
    half = mine_ref.shape[1]
    for out_ref, group in ((mine_ref, here), (other_ref, 1 - here)):
        columns = pl.ds(pl.multiple_of(group * half, 128), half)
        out_ref[...] = jnp.dot(
            heads_ref[...], w_ref[:, columns], preferred_element_type=jnp.float32
        ).astype(jnp.bfloat16)


def spatial_attention(query, key, value, weight):
    patches, cols = query.shape
    half = weight.shape[1] // 2
    whole = lambda i: (0, 0)
    block = lambda i: (i, 0)
    return pl.pallas_call(
        spatial_kernel,
        grid=(patches // ROWS,),
        in_specs=[
            pl.BlockSpec((ROWS, cols), block),
            pl.BlockSpec((patches, cols), whole),
            pl.BlockSpec((patches, cols), whole),
            pl.BlockSpec(weight.shape, whole),
        ],
        out_specs=[pl.BlockSpec((ROWS, half), block)] * 2,
        out_shape=[jax.ShapeDtypeStruct((patches, half), jnp.bfloat16)] * 2,
        scratch_shapes=[pltpu.VMEM((ROWS, cols), jnp.bfloat16)],
        compiler_params=pltpu.CompilerParams(vmem_limit_bytes=48 * MIB),
        name="spatial",
    )(query, key, value, weight)


def temporal_kernel(
    mid_mine, mid_other, gain_ref, w_ref, out_w_ref, mine_ref, other_ref, qkv_ref, heads_ref
):
    here = lax.axis_index("mp")
    frames_all, rows, half = mid_mine.shape
    total = frames_all * rows
    model = 2 * half
    pair = [
        (ref[...].reshape(total, half).astype(jnp.float32), pl.multiple_of(group * half, 128))
        for ref, group in ((mid_mine, here), (mid_other, 1 - here))
    ]
    mean = sum(jnp.sum(part, axis=-1, keepdims=True) for part, _ in pair) / model
    pair = [(part - mean, first) for part, first in pair]
    spread = sum(jnp.sum(part * part, axis=-1, keepdims=True) for part, _ in pair) / model
    scale = lax.rsqrt(spread + 1e-06)
    pair = [
        (
            (part * scale * gain_ref[:, pl.ds(first, half)].astype(jnp.float32)).astype(
                jnp.bfloat16
            ),
            first,
        )
        for part, first in pair
    ]
    for which in range(3):
        qkv_ref[which] = sum(
            jnp.dot(part, w_ref[which, pl.ds(first, half), :], preferred_element_type=jnp.float32)
            for part, first in pair
        ).astype(jnp.bfloat16)
    row_patch = lax.broadcasted_iota(jnp.int32, (total, total), 0) % rows
    col_patch = lax.broadcasted_iota(jnp.int32, (total, total), 1) % rows
    cols = qkv_ref.shape[2]
    head_attention(
        qkv_ref[0],
        lambda first, width: qkv_ref[1, :, first : first + width],
        lambda first, width: qkv_ref[2, :, first : first + width],
        heads_ref,
        slice(None),
        cols // HD,
        row_patch == col_patch,
    )
    for out_ref, group in ((mine_ref, here), (other_ref, 1 - here)):
        columns = pl.ds(pl.multiple_of(group * half, 128), half)
        out_ref[...] = (
            jnp.dot(heads_ref[...], out_w_ref[:, columns], preferred_element_type=jnp.float32)
            .astype(jnp.bfloat16)
            .reshape(frames_all, rows, half)
        )


def temporal_attention(mid_mine, mid_other, gain, weights, out_weight):
    frames_all, patch_rows, half = mid_mine.shape
    cols = weights.shape[2]
    total = frames_all * PATCHES
    block = pl.BlockSpec((frames_all, PATCHES, half), lambda i: (0, i, 0))
    return pl.pallas_call(
        temporal_kernel,
        grid=(patch_rows // PATCHES,),
        in_specs=[
            block,
            block,
            pl.BlockSpec((1, 2 * half), lambda i: (0, 0)),
            pl.BlockSpec(weights.shape, lambda i: (0, 0, 0)),
            pl.BlockSpec(out_weight.shape, lambda i: (0, 0)),
        ],
        out_specs=[block, block],
        out_shape=[jax.ShapeDtypeStruct(mid_mine.shape, jnp.bfloat16)] * 2,
        scratch_shapes=[
            pltpu.VMEM((3, total, cols), jnp.bfloat16),
            pltpu.VMEM((total, cols), jnp.bfloat16),
        ],
        compiler_params=pltpu.CompilerParams(vmem_limit_bytes=48 * MIB),
        name="temporal",
    )(mid_mine, mid_other, gain.reshape(1, -1), weights, out_weight)


def swap(values):
    return lax.ppermute(values, "mp", [(0, 1), (1, 0)])


def added(base, mine, other):
    update = mine.astype(jnp.float32) + other.astype(jnp.float32)
    return (base.astype(jnp.float32) + update).astype(jnp.bfloat16)


def on_device_pair(
    stream,
    spatial_qkv,
    spatial_out_w,
    temporal_gain,
    temporal_qkv_w,
    temporal_out_w,
    decoder_gain,
    decoder_kv_w,
    vertex_queries,
    crop_counts,
    crop_tiles,
    crop_owner,
):
    patches = stream.shape[1]
    half = stream.shape[2] // 2
    frames_all = crop_owner.shape[0]
    here = lax.axis_index("mp")
    mine, theirs = spatial_attention(
        spatial_qkv[0, :, 0], spatial_qkv[0, :, 1], spatial_qkv[0, :, 2], spatial_out_w
    )
    stream_half = lax.dynamic_slice_in_dim(stream[0], here * half, half, 1)
    middle = added(stream_half, mine, swap(theirs))
    mid_mine = lax.all_to_all(
        middle.reshape(frames_all, patches // frames_all, half),
        "frame",
        split_axis=0,
        concat_axis=0,
        tiled=True,
    )
    mid_other = swap(mid_mine)
    mine, theirs = temporal_attention(
        mid_mine, mid_other, temporal_gain, temporal_qkv_w, temporal_out_w
    )
    final_mine = added(mid_mine, mine, swap(theirs))
    stream_part = lax.all_to_all(
        final_mine, "frame", split_axis=0, concat_axis=0, tiled=True
    ).reshape(1, patches, half)
    frame_id = lax.axis_index("frame")
    my_tiles = lax.dynamic_index_in_dim(crop_tiles, frame_id, 0, keepdims=False)
    tile_view = stream_part.reshape(patches // TILE, TILE, half)
    crop_mine = jnp.take(tile_view, my_tiles, axis=0).reshape(MAXC * TILE, half)
    crop_other = swap(crop_mine)
    crop_rows = jnp.where(
        here == 0,
        jnp.concatenate([crop_mine, crop_other], axis=1),
        jnp.concatenate([crop_other, crop_mine], axis=1),
    )
    crop_norm = layer_norm(crop_rows.astype(jnp.float32), decoder_gain)
    return decode(
        crop_norm, decoder_kv_w, vertex_queries, crop_counts, crop_owner
    ), stream_part


def decode(crop_norm, decoder_kv_w, vertex_queries, crop_counts, crop_owner):
    frame_id = lax.axis_index("frame")
    frames_all = crop_owner.shape[0]
    dec_local = decoder_kv_w.shape[2]
    crop_keys = jnp.dot(crop_norm, decoder_kv_w[0], preferred_element_type=jnp.float32).astype(
        jnp.bfloat16
    )
    crop_values = jnp.dot(crop_norm, decoder_kv_w[1], preferred_element_type=jnp.float32).astype(
        jnp.bfloat16
    )
    crop_pairs = jnp.concatenate([crop_keys, crop_values], axis=1).reshape(
        MAXC, TILE, 2 * dec_local
    )
    live_slots, slot_index = crop_slots(crop_counts, crop_owner)
    targets = frame_id * RCAP + jnp.arange(RCAP, dtype=jnp.int32)
    choose = ((slot_index[None, :] == targets[:, None]) & live_slots[None, :]).astype(jnp.float32)
    my_owner = lax.dynamic_index_in_dim(crop_owner, frame_id, 0, keepdims=False)
    my_count = lax.dynamic_index_in_dim(crop_counts, frame_id, 0, keepdims=False)
    my_live = jnp.arange(MAXC, dtype=jnp.int32) < my_count
    to_owner = (
        (my_owner[None, :] == jnp.arange(frames_all, dtype=jnp.int32)[:, None]) & my_live[None, :]
    ).astype(jnp.bfloat16)
    outgoing = jnp.einsum(
        "nm,mtc->ntc", to_owner, crop_pairs, preferred_element_type=jnp.float32
    ).astype(jnp.bfloat16)
    incoming = lax.all_to_all(outgoing, "frame", split_axis=0, concat_axis=0, tiled=True)
    by_frame = choose.reshape(RCAP, frames_all, MAXC).sum(axis=2).astype(jnp.bfloat16)
    slot_pairs = jnp.einsum(
        "rg,gtc->rtc", by_frame, incoming, preferred_element_type=jnp.float32
    ).astype(jnp.bfloat16)
    heads_dec = dec_local // DEC_HD
    slot_keys = slot_pairs[:, :, :dec_local].reshape(RCAP, TILE, heads_dec, DEC_HD)
    slot_values = slot_pairs[:, :, dec_local:].reshape(RCAP, TILE, heads_dec, DEC_HD)
    queries = vertex_queries.reshape(V, heads_dec, DEC_HD)
    vertex_scores = jnp.einsum(
        "vhd,rthd->rhvt", queries, slot_keys, preferred_element_type=jnp.float32
    ) * DEC_HD ** (-0.5)
    vertex_weights = soft_weights(vertex_scores)
    decoded = jnp.einsum(
        "rhvt,rthd->rhdv", vertex_weights, slot_values, preferred_element_type=jnp.float32
    )
    return decoded.astype(jnp.bfloat16).reshape(RCAP, dec_local, V)


def solution(mesh):
    placed = (
        P("frame", None, None),
        P("frame", None, None, "mp"),
        P("mp", None),
        P(),
        P(None, None, "mp"),
        P("mp", None),
        P(),
        P(None, None, "mp"),
        P(None, "mp"),
        P(),
        P(),
        P(),
    )
    return jax.shard_map(
        on_device_pair if mesh.shape["mp"] == 2 else on_device_any,
        mesh=mesh,
        in_specs=placed,
        out_specs=(P("frame", "mp", None), P("frame", None, "mp")),
        check_vma=False,
    )
```

```python
import functools

import jax
import jax.numpy as jnp
from jax import lax
from jax.experimental import pallas as pl
from jax.experimental.pallas import tpu as pltpu
from jax.sharding import PartitionSpec as P

HD = 80
TILE = 128
MAXC = 3
RCAP = 4
DEC_HD = 64
V = 778
ROWS = 256
PATCHES = 16
CHUNKS = 2
LOG2E = 1.4426950408889634
MIB = 1 << 20


def layer_norm(values, gain_row):
    row_mean = jnp.mean(values, axis=-1, keepdims=True)
    centred = values - row_mean
    spread = jnp.mean(centred * centred, axis=-1, keepdims=True)
    return (centred * lax.rsqrt(spread + 1e-06) * gain_row.astype(jnp.float32)).astype(jnp.bfloat16)


def soft_weights(scores):
    row_top = jnp.max(scores, axis=-1, keepdims=True)
    raised = jnp.exp(scores - row_top)
    return (raised / jnp.sum(raised, axis=-1, keepdims=True)).astype(jnp.bfloat16)


def crop_slots(crop_counts, crop_owner):
    frames_all, most = crop_owner.shape
    live_slots = (jnp.arange(most, dtype=jnp.int32)[None, :] < crop_counts[:, None]).reshape(-1)
    owner_flat = crop_owner.reshape(-1)
    owner_hits = (
        (owner_flat[:, None] == jnp.arange(frames_all, dtype=jnp.int32)[None, :])
        & live_slots[:, None]
    ).astype(jnp.int32)
    before = jnp.cumsum(owner_hits, axis=0) - owner_hits
    slot_rank = jnp.sum(before * owner_hits, axis=1)
    return (live_slots, owner_flat * RCAP + slot_rank)


def on_device_any(
    stream,
    spatial_qkv,
    spatial_out_w,
    temporal_gain,
    temporal_qkv_w,
    temporal_out_w,
    decoder_gain,
    decoder_kv_w,
    vertex_queries,
    crop_counts,
    crop_tiles,
    crop_owner,
):
    patches = stream.shape[1]
    model_width = stream.shape[2]
    local_cols = spatial_qkv.shape[3]
    heads_here = local_cols // HD
    score_scale = HD ** (-0.5)
    spatial_query = spatial_qkv[0, :, 0].reshape(patches, heads_here, HD)
    spatial_key = spatial_qkv[0, :, 1].reshape(patches, heads_here, HD)
    spatial_value = spatial_qkv[0, :, 2].reshape(patches, heads_here, HD)
    scores = (
        jnp.einsum("qhd,khd->hqk", spatial_query, spatial_key, preferred_element_type=jnp.float32)
        * score_scale
    )
    weights = soft_weights(scores)
    spatial_heads = (
        jnp.einsum("hqk,khd->qhd", weights, spatial_value, preferred_element_type=jnp.float32)
        .astype(jnp.bfloat16)
        .reshape(patches, local_cols)
    )
    spatial_part = jnp.dot(spatial_heads, spatial_out_w, preferred_element_type=jnp.float32)
    spatial_total = lax.psum(spatial_part.astype(jnp.bfloat16), "mp").astype(jnp.float32)
    middle = (stream[0].astype(jnp.float32) + spatial_total).astype(jnp.bfloat16)
    normed = layer_norm(middle.astype(jnp.float32), temporal_gain)
    projected = jnp.stack(
        [
            jnp.dot(normed, temporal_qkv_w[which], preferred_element_type=jnp.float32).astype(
                jnp.bfloat16
            )
            for which in range(3)
        ],
        axis=1,
    )[None]
    gathered = lax.all_to_all(projected, "frame", split_axis=1, concat_axis=0, tiled=True)
    frames_all = gathered.shape[0]
    patch_rows = gathered.shape[1]
    temporal_query = gathered[:, :, 0].reshape(frames_all, patch_rows, heads_here, HD)
    temporal_key = gathered[:, :, 1].reshape(frames_all, patch_rows, heads_here, HD)
    temporal_value = gathered[:, :, 2].reshape(frames_all, patch_rows, heads_here, HD)
    frame_scores = (
        jnp.einsum(
            "fphd,gphd->phfg", temporal_query, temporal_key, preferred_element_type=jnp.float32
        )
        * score_scale
    )
    frame_weights = soft_weights(frame_scores)
    mixed_heads = (
        jnp.einsum(
            "phfg,gphd->fphd", frame_weights, temporal_value, preferred_element_type=jnp.float32
        )
        .astype(jnp.bfloat16)
        .reshape(frames_all, patch_rows, local_cols)
    )
    frame_heads = lax.all_to_all(mixed_heads, "frame", split_axis=0, concat_axis=1, tiled=True)
    temporal_part = jnp.dot(frame_heads[0], temporal_out_w, preferred_element_type=jnp.float32)
    temporal_total = lax.psum(temporal_part.astype(jnp.bfloat16), "mp").astype(jnp.float32)
    final_stream = (middle.astype(jnp.float32) + temporal_total).astype(jnp.bfloat16)
    out_cols = model_width // lax.axis_size("mp")
    stream_part = lax.dynamic_slice_in_dim(
        final_stream, lax.axis_index("mp") * out_cols, out_cols, 1
    )[None]
    frame_id = lax.axis_index("frame")
    my_tiles = lax.dynamic_index_in_dim(crop_tiles, frame_id, 0, keepdims=False)
    tile_view = final_stream.reshape(patches // TILE, TILE, model_width)
    crop_rows = jnp.take(tile_view, my_tiles, axis=0)
    crop_norm = layer_norm(crop_rows.astype(jnp.float32), decoder_gain).reshape(
        MAXC * TILE, model_width
    )
    return decode(
        crop_norm, decoder_kv_w, vertex_queries, crop_counts, crop_owner
    ), stream_part


def head_window(head):
    first = head * HD // 128 * 128
    last = -(-(head + 1) * HD // 128) * 128
    return first, last - first, head * HD - first


def head_attention(query, key_of, value_of, out_ref, row_slice, heads_here, keep):
    factor = HD ** (-0.5) * LOG2E
    done = {}
    for head in range(heads_here):
        first, width, start = head_window(head)
        lane = lax.broadcasted_iota(jnp.int32, (1, width), 1)
        inside = (lane >= start) & (lane < start + HD)
        q_here = query[:, first : first + width]
        q_here = jnp.where(inside, q_here, jnp.zeros_like(q_here))
        scores = lax.dot_general(
            q_here,
            key_of(first, width),
            (((1,), (1,)), ((), ())),
            preferred_element_type=jnp.float32,
        )
        if keep is not None:
            scores = jnp.where(keep, scores, -jnp.inf)
        top = jnp.max(scores, axis=-1, keepdims=True)
        raised = jnp.exp2(scores * factor - top * factor).astype(jnp.bfloat16)
        v_here = value_of(first, width)
        v_here = jnp.where(inside, v_here, jnp.ones_like(v_here))
        both = jnp.dot(raised, v_here, preferred_element_type=jnp.float32)
        at = 0 if start else width - 1
        found = (both / both[:, at : at + 1]).astype(jnp.bfloat16)
        for tile in range(width // 128):
            column = first + tile * 128
            part = found[:, tile * 128 : tile * 128 + 128]
            if column in done:
                part = jnp.where(inside[:, tile * 128 : tile * 128 + 128], part, done[column])
            done[column] = part
    for column, part in done.items():
        out_ref[row_slice, column : column + 128] = part


def spatial_kernel(q_ref, k_ref, v_ref, w_ref, mine_ref, other_ref, heads_ref):
    here = lax.axis_index("mp")
    cols = q_ref.shape[1]
    head_attention(
        q_ref[...],
        lambda first, width: k_ref[:, first : first + width],
        lambda first, width: v_ref[:, first : first + width],
        heads_ref,
        slice(None),
        cols // HD,
        None,
    )
    half = mine_ref.shape[1]
    for out_ref, group in ((mine_ref, here), (other_ref, 1 - here)):
        columns = pl.ds(pl.multiple_of(group * half, 128), half)
        out_ref[...] = jnp.dot(
            heads_ref[...], w_ref[:, columns], preferred_element_type=jnp.float32
        ).astype(jnp.bfloat16)


def spatial_attention(query, key, value, weight):
    patches, cols = query.shape
    half = weight.shape[1] // 2
    whole = lambda i: (0, 0)
    block = lambda i: (i, 0)
    return pl.pallas_call(
        spatial_kernel,
        grid=(patches // ROWS,),
        in_specs=[
            pl.BlockSpec((ROWS, cols), block),
            pl.BlockSpec(key.shape, whole),
            pl.BlockSpec(key.shape, whole),
            pl.BlockSpec(weight.shape, whole),
        ],
        out_specs=[pl.BlockSpec((ROWS, half), block)] * 2,
        out_shape=[jax.ShapeDtypeStruct((patches, half), jnp.bfloat16)] * 2,
        scratch_shapes=[pltpu.VMEM((ROWS, cols), jnp.bfloat16)],
        compiler_params=pltpu.CompilerParams(vmem_limit_bytes=48 * MIB),
        name="spatial",
    )(query, key, value, weight)


def temporal_kernel(
    mid_mine, mid_other, gain_ref, w_ref, out_w_ref, mine_ref, other_ref, qkv_ref, heads_ref
):
    here = lax.axis_index("mp")
    frames_all, rows, half = mid_mine.shape
    total = frames_all * rows
    model = 2 * half
    pair = [
        (ref[...].reshape(total, half).astype(jnp.float32), pl.multiple_of(group * half, 128))
        for ref, group in ((mid_mine, here), (mid_other, 1 - here))
    ]
    mean = sum(jnp.sum(part, axis=-1, keepdims=True) for part, _ in pair) / model
    pair = [(part - mean, first) for part, first in pair]
    spread = sum(jnp.sum(part * part, axis=-1, keepdims=True) for part, _ in pair) / model
    scale = lax.rsqrt(spread + 1e-06)
    pair = [
        (
            (part * scale * gain_ref[:, pl.ds(first, half)].astype(jnp.float32)).astype(
                jnp.bfloat16
            ),
            first,
        )
        for part, first in pair
    ]
    for which in range(3):
        qkv_ref[which] = sum(
            jnp.dot(part, w_ref[which, pl.ds(first, half), :], preferred_element_type=jnp.float32)
            for part, first in pair
        ).astype(jnp.bfloat16)
    row_patch = lax.broadcasted_iota(jnp.int32, (total, total), 0) % rows
    col_patch = lax.broadcasted_iota(jnp.int32, (total, total), 1) % rows
    cols = qkv_ref.shape[2]
    head_attention(
        qkv_ref[0],
        lambda first, width: qkv_ref[1, :, first : first + width],
        lambda first, width: qkv_ref[2, :, first : first + width],
        heads_ref,
        slice(None),
        cols // HD,
        row_patch == col_patch,
    )
    for out_ref, group in ((mine_ref, here), (other_ref, 1 - here)):
        columns = pl.ds(pl.multiple_of(group * half, 128), half)
        out_ref[...] = (
            jnp.dot(heads_ref[...], out_w_ref[:, columns], preferred_element_type=jnp.float32)
            .astype(jnp.bfloat16)
            .reshape(frames_all, rows, half)
        )


def temporal_attention(mid_mine, mid_other, gain, weights, out_weight):
    frames_all, patch_rows, half = mid_mine.shape
    cols = weights.shape[2]
    total = frames_all * PATCHES
    block = pl.BlockSpec((frames_all, PATCHES, half), lambda i: (0, i, 0))
    return pl.pallas_call(
        temporal_kernel,
        grid=(patch_rows // PATCHES,),
        in_specs=[
            block,
            block,
            pl.BlockSpec((1, 2 * half), lambda i: (0, 0)),
            pl.BlockSpec(weights.shape, lambda i: (0, 0, 0)),
            pl.BlockSpec(out_weight.shape, lambda i: (0, 0)),
        ],
        out_specs=[block, block],
        out_shape=[jax.ShapeDtypeStruct(mid_mine.shape, jnp.bfloat16)] * 2,
        scratch_shapes=[
            pltpu.VMEM((3, total, cols), jnp.bfloat16),
            pltpu.VMEM((total, cols), jnp.bfloat16),
        ],
        compiler_params=pltpu.CompilerParams(vmem_limit_bytes=48 * MIB),
        name="temporal",
    )(mid_mine, mid_other, gain.reshape(1, -1), weights, out_weight)


def swap(values):
    return lax.ppermute(values, "mp", [(0, 1), (1, 0)])


def added(base, mine, other):
    update = mine.astype(jnp.float32) + other.astype(jnp.float32)
    return (base.astype(jnp.float32) + update).astype(jnp.bfloat16)


def on_device_pair(
    stream,
    spatial_qkv,
    spatial_out_w,
    temporal_gain,
    temporal_qkv_w,
    temporal_out_w,
    decoder_gain,
    decoder_kv_w,
    vertex_queries,
    crop_counts,
    crop_tiles,
    crop_owner,
):
    patches = stream.shape[1]
    half = stream.shape[2] // 2
    frames_all = crop_owner.shape[0]
    here = lax.axis_index("mp")
    own_rows = patches // frames_all
    part_rows = own_rows // CHUNKS

    def chunk_of(values, chunk):
        split = values.reshape(frames_all, CHUNKS, part_rows, values.shape[1])
        return split[:, chunk].reshape(frames_all * part_rows, values.shape[1])

    key, value = spatial_qkv[0, :, 1], spatial_qkv[0, :, 2]
    stream_half = lax.dynamic_slice_in_dim(stream[0], here * half, half, 1)
    arrived = []
    for chunk in range(CHUNKS):
        mine, theirs = spatial_attention(
            chunk_of(spatial_qkv[0, :, 0], chunk), key, value, spatial_out_w
        )
        middle = added(chunk_of(stream_half, chunk), mine, swap(theirs))
        arrived.append(
            lax.all_to_all(
                middle.reshape(frames_all, part_rows, half),
                "frame",
                split_axis=0,
                concat_axis=0,
                tiled=True,
            )
        )
    returned = []
    for mid_mine in arrived:
        mine, theirs = temporal_attention(
            mid_mine, swap(mid_mine), temporal_gain, temporal_qkv_w, temporal_out_w
        )
        final_mine = added(mid_mine, mine, swap(theirs))
        returned.append(
            lax.all_to_all(final_mine, "frame", split_axis=0, concat_axis=0, tiled=True)
        )
    stream_part = jnp.stack(returned, axis=1).reshape(1, patches, half)
    frame_id = lax.axis_index("frame")
    my_tiles = lax.dynamic_index_in_dim(crop_tiles, frame_id, 0, keepdims=False)
    tile_view = stream_part.reshape(patches // TILE, TILE, half)
    crop_mine = jnp.take(tile_view, my_tiles, axis=0).reshape(MAXC * TILE, half)
    crop_other = swap(crop_mine)
    crop_rows = jnp.where(
        here == 0,
        jnp.concatenate([crop_mine, crop_other], axis=1),
        jnp.concatenate([crop_other, crop_mine], axis=1),
    )
    crop_norm = layer_norm(crop_rows.astype(jnp.float32), decoder_gain)
    return decode(
        crop_norm, decoder_kv_w, vertex_queries, crop_counts, crop_owner
    ), stream_part


def decode(crop_norm, decoder_kv_w, vertex_queries, crop_counts, crop_owner):
    frame_id = lax.axis_index("frame")
    frames_all = crop_owner.shape[0]
    dec_local = decoder_kv_w.shape[2]
    crop_keys = jnp.dot(crop_norm, decoder_kv_w[0], preferred_element_type=jnp.float32).astype(
        jnp.bfloat16
    )
    crop_values = jnp.dot(crop_norm, decoder_kv_w[1], preferred_element_type=jnp.float32).astype(
        jnp.bfloat16
    )
    crop_pairs = jnp.concatenate([crop_keys, crop_values], axis=1).reshape(
        MAXC, TILE, 2 * dec_local
    )
    live_slots, slot_index = crop_slots(crop_counts, crop_owner)
    targets = frame_id * RCAP + jnp.arange(RCAP, dtype=jnp.int32)
    choose = ((slot_index[None, :] == targets[:, None]) & live_slots[None, :]).astype(jnp.float32)
    my_owner = lax.dynamic_index_in_dim(crop_owner, frame_id, 0, keepdims=False)
    my_count = lax.dynamic_index_in_dim(crop_counts, frame_id, 0, keepdims=False)
    my_live = jnp.arange(MAXC, dtype=jnp.int32) < my_count
    to_owner = (
        (my_owner[None, :] == jnp.arange(frames_all, dtype=jnp.int32)[:, None]) & my_live[None, :]
    ).astype(jnp.bfloat16)
    outgoing = jnp.einsum(
        "nm,mtc->ntc", to_owner, crop_pairs, preferred_element_type=jnp.float32
    ).astype(jnp.bfloat16)
    incoming = lax.all_to_all(outgoing, "frame", split_axis=0, concat_axis=0, tiled=True)
    by_frame = choose.reshape(RCAP, frames_all, MAXC).sum(axis=2).astype(jnp.bfloat16)
    slot_pairs = jnp.einsum(
        "rg,gtc->rtc", by_frame, incoming, preferred_element_type=jnp.float32
    ).astype(jnp.bfloat16)
    if dec_local % 128 == 0:
        return vertex_decoder(slot_pairs, vertex_queries)
    heads_dec = dec_local // DEC_HD
    slot_keys = slot_pairs[:, :, :dec_local].reshape(RCAP, TILE, heads_dec, DEC_HD)
    slot_values = slot_pairs[:, :, dec_local:].reshape(RCAP, TILE, heads_dec, DEC_HD)
    queries = vertex_queries.reshape(V, heads_dec, DEC_HD)
    vertex_scores = jnp.einsum(
        "vhd,rthd->rhvt", queries, slot_keys, preferred_element_type=jnp.float32
    ) * DEC_HD ** (-0.5)
    vertex_weights = soft_weights(vertex_scores)
    decoded = jnp.einsum(
        "rhvt,rthd->rhdv", vertex_weights, slot_values, preferred_element_type=jnp.float32
    )
    return decoded.astype(jnp.bfloat16).reshape(RCAP, dec_local, V)


def decoder_kernel(pair_ref, query_ref, out_ref):
    width = query_ref.shape[1]
    factor = DEC_HD ** (-0.5) * LOG2E
    values = pair_ref[0, :, width:].T
    lane = lax.broadcasted_iota(jnp.int32, (1, 128), 1)
    for head in range(width // DEC_HD):
        start = head * DEC_HD
        first = start // 128 * 128
        inside = (lane >= start - first) & (lane < start - first + DEC_HD)
        keys = pair_ref[0, :, first : first + 128]
        keys = jnp.where(inside, keys, jnp.zeros_like(keys))
        scores = lax.dot_general(
            keys,
            query_ref[:, first : first + 128],
            (((1,), (1,)), ((), ())),
            preferred_element_type=jnp.float32,
        )
        top = jnp.max(scores, axis=0, keepdims=True)
        raised = jnp.exp2((scores - top) * factor)
        weights = (raised / jnp.sum(raised, axis=0, keepdims=True)).astype(jnp.bfloat16)
        out_ref[0, start : start + DEC_HD, :] = jnp.dot(
            values[start : start + DEC_HD], weights, preferred_element_type=jnp.float32
        ).astype(jnp.bfloat16)


def vertex_decoder(slot_pairs, queries):
    slots, keys, both = slot_pairs.shape
    vertices, width = queries.shape
    return pl.pallas_call(
        decoder_kernel,
        grid=(slots,),
        in_specs=[
            pl.BlockSpec((1, keys, both), lambda i: (i, 0, 0)),
            pl.BlockSpec((vertices, width), lambda i: (0, 0)),
        ],
        out_specs=pl.BlockSpec((1, width, vertices), lambda i: (i, 0, 0)),
        out_shape=jax.ShapeDtypeStruct((slots, width, vertices), jnp.bfloat16),
        compiler_params=pltpu.CompilerParams(vmem_limit_bytes=32 * MIB),
        name="decoder",
    )(slot_pairs, queries)


def solution(mesh):
    placed = (
        P("frame", None, None),
        P("frame", None, None, "mp"),
        P("mp", None),
        P(),
        P(None, None, "mp"),
        P("mp", None),
        P(),
        P(None, None, "mp"),
        P(None, "mp"),
        P(),
        P(),
        P(),
    )
    return jax.shard_map(
        on_device_pair if mesh.shape["mp"] == 2 else on_device_any,
        mesh=mesh,
        in_specs=placed,
        out_specs=(P("frame", "mp", None), P("frame", None, "mp")),
        check_vma=False,
    )
```

```python
import functools

import jax
import jax.numpy as jnp
from jax import lax
from jax.experimental import pallas as pl
from jax.experimental.pallas import tpu as pltpu
from jax.sharding import PartitionSpec as P

HD = 80
TILE = 128
MAXC = 3
RCAP = 4
DEC_HD = 64
V = 778
ROWS = 256
PATCHES = 16
CHUNKS = 2
LOG2E = 1.4426950408889634
MIB = 1 << 20


def layer_norm(values, gain_row):
    row_mean = jnp.mean(values, axis=-1, keepdims=True)
    centred = values - row_mean
    spread = jnp.mean(centred * centred, axis=-1, keepdims=True)
    return (centred * lax.rsqrt(spread + 1e-06) * gain_row.astype(jnp.float32)).astype(jnp.bfloat16)


def soft_weights(scores):
    row_top = jnp.max(scores, axis=-1, keepdims=True)
    raised = jnp.exp(scores - row_top)
    return (raised / jnp.sum(raised, axis=-1, keepdims=True)).astype(jnp.bfloat16)


def crop_slots(crop_counts, crop_owner):
    frames_all, most = crop_owner.shape
    live_slots = (jnp.arange(most, dtype=jnp.int32)[None, :] < crop_counts[:, None]).reshape(-1)
    owner_flat = crop_owner.reshape(-1)
    owner_hits = (
        (owner_flat[:, None] == jnp.arange(frames_all, dtype=jnp.int32)[None, :])
        & live_slots[:, None]
    ).astype(jnp.int32)
    before = jnp.cumsum(owner_hits, axis=0) - owner_hits
    slot_rank = jnp.sum(before * owner_hits, axis=1)
    return (live_slots, owner_flat * RCAP + slot_rank)


def on_device_any(
    stream,
    spatial_qkv,
    spatial_out_w,
    temporal_gain,
    temporal_qkv_w,
    temporal_out_w,
    decoder_gain,
    decoder_kv_w,
    vertex_queries,
    crop_counts,
    crop_tiles,
    crop_owner,
):
    patches = stream.shape[1]
    model_width = stream.shape[2]
    local_cols = spatial_qkv.shape[3]
    heads_here = local_cols // HD
    score_scale = HD ** (-0.5)
    spatial_query = spatial_qkv[0, :, 0].reshape(patches, heads_here, HD)
    spatial_key = spatial_qkv[0, :, 1].reshape(patches, heads_here, HD)
    spatial_value = spatial_qkv[0, :, 2].reshape(patches, heads_here, HD)
    scores = (
        jnp.einsum("qhd,khd->hqk", spatial_query, spatial_key, preferred_element_type=jnp.float32)
        * score_scale
    )
    weights = soft_weights(scores)
    spatial_heads = (
        jnp.einsum("hqk,khd->qhd", weights, spatial_value, preferred_element_type=jnp.float32)
        .astype(jnp.bfloat16)
        .reshape(patches, local_cols)
    )
    spatial_part = jnp.dot(spatial_heads, spatial_out_w, preferred_element_type=jnp.float32)
    spatial_total = lax.psum(spatial_part.astype(jnp.bfloat16), "mp").astype(jnp.float32)
    middle = (stream[0].astype(jnp.float32) + spatial_total).astype(jnp.bfloat16)
    normed = layer_norm(middle.astype(jnp.float32), temporal_gain)
    projected = jnp.stack(
        [
            jnp.dot(normed, temporal_qkv_w[which], preferred_element_type=jnp.float32).astype(
                jnp.bfloat16
            )
            for which in range(3)
        ],
        axis=1,
    )[None]
    gathered = lax.all_to_all(projected, "frame", split_axis=1, concat_axis=0, tiled=True)
    frames_all = gathered.shape[0]
    patch_rows = gathered.shape[1]
    temporal_query = gathered[:, :, 0].reshape(frames_all, patch_rows, heads_here, HD)
    temporal_key = gathered[:, :, 1].reshape(frames_all, patch_rows, heads_here, HD)
    temporal_value = gathered[:, :, 2].reshape(frames_all, patch_rows, heads_here, HD)
    frame_scores = (
        jnp.einsum(
            "fphd,gphd->phfg", temporal_query, temporal_key, preferred_element_type=jnp.float32
        )
        * score_scale
    )
    frame_weights = soft_weights(frame_scores)
    mixed_heads = (
        jnp.einsum(
            "phfg,gphd->fphd", frame_weights, temporal_value, preferred_element_type=jnp.float32
        )
        .astype(jnp.bfloat16)
        .reshape(frames_all, patch_rows, local_cols)
    )
    frame_heads = lax.all_to_all(mixed_heads, "frame", split_axis=0, concat_axis=1, tiled=True)
    temporal_part = jnp.dot(frame_heads[0], temporal_out_w, preferred_element_type=jnp.float32)
    temporal_total = lax.psum(temporal_part.astype(jnp.bfloat16), "mp").astype(jnp.float32)
    final_stream = (middle.astype(jnp.float32) + temporal_total).astype(jnp.bfloat16)
    out_cols = model_width // lax.axis_size("mp")
    stream_part = lax.dynamic_slice_in_dim(
        final_stream, lax.axis_index("mp") * out_cols, out_cols, 1
    )[None]
    frame_id = lax.axis_index("frame")
    my_tiles = lax.dynamic_index_in_dim(crop_tiles, frame_id, 0, keepdims=False)
    tile_view = final_stream.reshape(patches // TILE, TILE, model_width)
    crop_rows = jnp.take(tile_view, my_tiles, axis=0)
    crop_norm = layer_norm(crop_rows.astype(jnp.float32), decoder_gain).reshape(
        MAXC * TILE, model_width
    )
    return decode(
        [crop_norm], decoder_kv_w, vertex_queries, crop_counts, crop_owner
    ), stream_part


def head_window(head):
    first = head * HD // 128 * 128
    last = -(-(head + 1) * HD // 128) * 128
    return first, last - first, head * HD - first


def head_attention(query, key_of, value_of, out_ref, row_slice, heads_here, keep):
    factor = HD ** (-0.5) * LOG2E
    done = {}
    for head in range(heads_here):
        first, width, start = head_window(head)
        lane = lax.broadcasted_iota(jnp.int32, (1, width), 1)
        inside = (lane >= start) & (lane < start + HD)
        q_here = query[:, first : first + width]
        q_here = jnp.where(inside, q_here, jnp.zeros_like(q_here))
        scores = lax.dot_general(
            q_here,
            key_of(first, width),
            (((1,), (1,)), ((), ())),
            preferred_element_type=jnp.float32,
        )
        if keep is not None:
            scores = jnp.where(keep, scores, -jnp.inf)
        top = jnp.max(scores, axis=-1, keepdims=True)
        raised = jnp.exp2(scores * factor - top * factor).astype(jnp.bfloat16)
        v_here = value_of(first, width)
        v_here = jnp.where(inside, v_here, jnp.ones_like(v_here))
        both = jnp.dot(raised, v_here, preferred_element_type=jnp.float32)
        at = 0 if start else width - 1
        found = (both / both[:, at : at + 1]).astype(jnp.bfloat16)
        for tile in range(width // 128):
            column = first + tile * 128
            part = found[:, tile * 128 : tile * 128 + 128]
            if column in done:
                part = jnp.where(inside[:, tile * 128 : tile * 128 + 128], part, done[column])
            done[column] = part
    for column, part in done.items():
        out_ref[row_slice, column : column + 128] = part


def spatial_kernel(q_ref, k_ref, v_ref, w_ref, mine_ref, other_ref, heads_ref):
    here = lax.axis_index("mp")
    cols = q_ref.shape[1]
    head_attention(
        q_ref[...],
        lambda first, width: k_ref[:, first : first + width],
        lambda first, width: v_ref[:, first : first + width],
        heads_ref,
        slice(None),
        cols // HD,
        None,
    )
    half = mine_ref.shape[1]
    for out_ref, group in ((mine_ref, here), (other_ref, 1 - here)):
        columns = pl.ds(pl.multiple_of(group * half, 128), half)
        out_ref[...] = jnp.dot(
            heads_ref[...], w_ref[:, columns], preferred_element_type=jnp.float32
        ).astype(jnp.bfloat16)


def spatial_attention(query, key, value, weight):
    patches, cols = query.shape
    half = weight.shape[1] // 2
    whole = lambda i: (0, 0)
    block = lambda i: (i, 0)
    return pl.pallas_call(
        spatial_kernel,
        grid=(patches // ROWS,),
        in_specs=[
            pl.BlockSpec((ROWS, cols), block),
            pl.BlockSpec(key.shape, whole),
            pl.BlockSpec(key.shape, whole),
            pl.BlockSpec(weight.shape, whole),
        ],
        out_specs=[pl.BlockSpec((ROWS, half), block)] * 2,
        out_shape=[jax.ShapeDtypeStruct((patches, half), jnp.bfloat16)] * 2,
        scratch_shapes=[pltpu.VMEM((ROWS, cols), jnp.bfloat16)],
        compiler_params=pltpu.CompilerParams(vmem_limit_bytes=48 * MIB),
        name="spatial",
    )(query, key, value, weight)


def temporal_kernel(
    mid_mine, mid_other, gain_ref, w_ref, out_w_ref, mine_ref, other_ref, qkv_ref, heads_ref
):
    here = lax.axis_index("mp")
    frames_all, rows, half = mid_mine.shape
    total = frames_all * rows
    model = 2 * half
    pair = [
        (ref[...].reshape(total, half).astype(jnp.float32), pl.multiple_of(group * half, 128))
        for ref, group in ((mid_mine, here), (mid_other, 1 - here))
    ]
    mean = sum(jnp.sum(part, axis=-1, keepdims=True) for part, _ in pair) / model
    pair = [(part - mean, first) for part, first in pair]
    spread = sum(jnp.sum(part * part, axis=-1, keepdims=True) for part, _ in pair) / model
    scale = lax.rsqrt(spread + 1e-06)
    pair = [
        (
            (part * scale * gain_ref[:, pl.ds(first, half)].astype(jnp.float32)).astype(
                jnp.bfloat16
            ),
            first,
        )
        for part, first in pair
    ]
    for which in range(3):
        qkv_ref[which] = sum(
            jnp.dot(part, w_ref[which, pl.ds(first, half), :], preferred_element_type=jnp.float32)
            for part, first in pair
        ).astype(jnp.bfloat16)
    row_patch = lax.broadcasted_iota(jnp.int32, (total, total), 0) % rows
    col_patch = lax.broadcasted_iota(jnp.int32, (total, total), 1) % rows
    cols = qkv_ref.shape[2]
    head_attention(
        qkv_ref[0],
        lambda first, width: qkv_ref[1, :, first : first + width],
        lambda first, width: qkv_ref[2, :, first : first + width],
        heads_ref,
        slice(None),
        cols // HD,
        row_patch == col_patch,
    )
    for out_ref, group in ((mine_ref, here), (other_ref, 1 - here)):
        columns = pl.ds(pl.multiple_of(group * half, 128), half)
        out_ref[...] = (
            jnp.dot(heads_ref[...], out_w_ref[:, columns], preferred_element_type=jnp.float32)
            .astype(jnp.bfloat16)
            .reshape(frames_all, rows, half)
        )


def temporal_attention(mid_mine, mid_other, gain, weights, out_weight):
    frames_all, patch_rows, half = mid_mine.shape
    cols = weights.shape[2]
    total = frames_all * PATCHES
    block = pl.BlockSpec((frames_all, PATCHES, half), lambda i: (0, i, 0))
    return pl.pallas_call(
        temporal_kernel,
        grid=(patch_rows // PATCHES,),
        in_specs=[
            block,
            block,
            pl.BlockSpec((1, 2 * half), lambda i: (0, 0)),
            pl.BlockSpec(weights.shape, lambda i: (0, 0, 0)),
            pl.BlockSpec(out_weight.shape, lambda i: (0, 0)),
        ],
        out_specs=[block, block],
        out_shape=[jax.ShapeDtypeStruct(mid_mine.shape, jnp.bfloat16)] * 2,
        scratch_shapes=[
            pltpu.VMEM((3, total, cols), jnp.bfloat16),
            pltpu.VMEM((total, cols), jnp.bfloat16),
        ],
        compiler_params=pltpu.CompilerParams(vmem_limit_bytes=48 * MIB),
        name="temporal",
    )(mid_mine, mid_other, gain.reshape(1, -1), weights, out_weight)


def swap(values):
    return lax.ppermute(values, "mp", [(0, 1), (1, 0)])


def added(base, mine, other):
    update = mine.astype(jnp.float32) + other.astype(jnp.float32)
    return (base.astype(jnp.float32) + update).astype(jnp.bfloat16)


def on_device_pair(
    stream,
    spatial_qkv,
    spatial_out_w,
    temporal_gain,
    temporal_qkv_w,
    temporal_out_w,
    decoder_gain,
    decoder_kv_w,
    vertex_queries,
    crop_counts,
    crop_tiles,
    crop_owner,
):
    patches = stream.shape[1]
    half = stream.shape[2] // 2
    frames_all = crop_owner.shape[0]
    here = lax.axis_index("mp")
    own_rows = patches // frames_all
    part_rows = own_rows // CHUNKS

    def chunk_of(values, chunk):
        split = values.reshape(frames_all, CHUNKS, part_rows, values.shape[1])
        return split[:, chunk].reshape(frames_all * part_rows, values.shape[1])

    key, value = spatial_qkv[0, :, 1], spatial_qkv[0, :, 2]
    stream_half = lax.dynamic_slice_in_dim(stream[0], here * half, half, 1)
    arrived = []
    for chunk in range(CHUNKS):
        mine, theirs = spatial_attention(
            chunk_of(spatial_qkv[0, :, 0], chunk), key, value, spatial_out_w
        )
        middle = added(chunk_of(stream_half, chunk), mine, swap(theirs))
        arrived.append(
            lax.all_to_all(
                middle.reshape(frames_all, part_rows, half),
                "frame",
                split_axis=0,
                concat_axis=0,
                tiled=True,
            )
        )
    returned = []
    for mid_mine in arrived:
        mine, theirs = temporal_attention(
            mid_mine, swap(mid_mine), temporal_gain, temporal_qkv_w, temporal_out_w
        )
        final_mine = added(mid_mine, mine, swap(theirs))
        returned.append(
            lax.all_to_all(final_mine, "frame", split_axis=0, concat_axis=0, tiled=True)
        )
    stream_part = jnp.stack(returned, axis=1).reshape(1, patches, half)
    frame_id = lax.axis_index("frame")
    my_tiles = lax.dynamic_index_in_dim(crop_tiles, frame_id, 0, keepdims=False)
    norms = []
    for part in returned:
        tile_view = part.reshape(patches // TILE, TILE // CHUNKS, half)
        crop_mine = jnp.concatenate(
            [
                lax.dynamic_index_in_dim(tile_view, my_tiles[slot], 0, keepdims=False)
                for slot in range(MAXC)
            ],
            axis=0,
        )
        crop_other = swap(crop_mine)
        crop_rows = jnp.where(
            here == 0,
            jnp.concatenate([crop_mine, crop_other], axis=1),
            jnp.concatenate([crop_other, crop_mine], axis=1),
        )
        norms.append(layer_norm(crop_rows.astype(jnp.float32), decoder_gain))
    return decode(norms, decoder_kv_w, vertex_queries, crop_counts, crop_owner), stream_part


def decode(crop_norms, decoder_kv_w, vertex_queries, crop_counts, crop_owner):
    frame_id = lax.axis_index("frame")
    frames_all = crop_owner.shape[0]
    dec_local = decoder_kv_w.shape[2]
    live_slots, slot_index = crop_slots(crop_counts, crop_owner)
    targets = frame_id * RCAP + jnp.arange(RCAP, dtype=jnp.int32)
    choose = ((slot_index[None, :] == targets[:, None]) & live_slots[None, :]).astype(jnp.float32)
    my_owner = lax.dynamic_index_in_dim(crop_owner, frame_id, 0, keepdims=False)
    my_count = lax.dynamic_index_in_dim(crop_counts, frame_id, 0, keepdims=False)
    my_live = jnp.arange(MAXC, dtype=jnp.int32) < my_count
    to_owner = (
        (my_owner[None, :] == jnp.arange(frames_all, dtype=jnp.int32)[:, None]) & my_live[None, :]
    ).astype(jnp.bfloat16)
    by_frame = choose.reshape(RCAP, frames_all, MAXC).sum(axis=2).astype(jnp.bfloat16)
    pieces = []
    for crop_norm in crop_norms:
        crop_keys = jnp.dot(crop_norm, decoder_kv_w[0], preferred_element_type=jnp.float32).astype(
            jnp.bfloat16
        )
        crop_values = jnp.dot(crop_norm, decoder_kv_w[1], preferred_element_type=jnp.float32).astype(
            jnp.bfloat16
        )
        crop_pairs = jnp.concatenate([crop_keys, crop_values], axis=1).reshape(
            MAXC, -1, 2 * dec_local
        )
        outgoing = jnp.einsum(
            "nm,mtc->ntc", to_owner, crop_pairs, preferred_element_type=jnp.float32
        ).astype(jnp.bfloat16)
        incoming = lax.all_to_all(outgoing, "frame", split_axis=0, concat_axis=0, tiled=True)
        piece = jnp.einsum(
            "rg,gtc->rtc", by_frame, incoming, preferred_element_type=jnp.float32
        ).astype(jnp.bfloat16)
        pieces.append(piece)
    slot_pairs = jnp.concatenate(pieces, axis=1)
    if dec_local % 128 == 0:
        return vertex_decoder(slot_pairs, vertex_queries)
    heads_dec = dec_local // DEC_HD
    slot_keys = slot_pairs[:, :, :dec_local].reshape(RCAP, TILE, heads_dec, DEC_HD)
    slot_values = slot_pairs[:, :, dec_local:].reshape(RCAP, TILE, heads_dec, DEC_HD)
    queries = vertex_queries.reshape(V, heads_dec, DEC_HD)
    vertex_scores = jnp.einsum(
        "vhd,rthd->rhvt", queries, slot_keys, preferred_element_type=jnp.float32
    ) * DEC_HD ** (-0.5)
    vertex_weights = soft_weights(vertex_scores)
    decoded = jnp.einsum(
        "rhvt,rthd->rhdv", vertex_weights, slot_values, preferred_element_type=jnp.float32
    )
    return decoded.astype(jnp.bfloat16).reshape(RCAP, dec_local, V)


def decoder_kernel(pair_ref, query_ref, out_ref):
    width = query_ref.shape[1]
    factor = DEC_HD ** (-0.5) * LOG2E
    values = pair_ref[0, :, width:].T
    lane = lax.broadcasted_iota(jnp.int32, (1, 128), 1)
    for head in range(width // DEC_HD):
        start = head * DEC_HD
        first = start // 128 * 128
        inside = (lane >= start - first) & (lane < start - first + DEC_HD)
        keys = pair_ref[0, :, first : first + 128]
        keys = jnp.where(inside, keys, jnp.zeros_like(keys))
        scores = lax.dot_general(
            keys,
            query_ref[:, first : first + 128],
            (((1,), (1,)), ((), ())),
            preferred_element_type=jnp.float32,
        )
        top = jnp.max(scores, axis=0, keepdims=True)
        raised = jnp.exp2((scores - top) * factor)
        weights = (raised / jnp.sum(raised, axis=0, keepdims=True)).astype(jnp.bfloat16)
        out_ref[0, start : start + DEC_HD, :] = jnp.dot(
            values[start : start + DEC_HD], weights, preferred_element_type=jnp.float32
        ).astype(jnp.bfloat16)


def vertex_decoder(slot_pairs, queries):
    slots, keys, both = slot_pairs.shape
    vertices, width = queries.shape
    return pl.pallas_call(
        decoder_kernel,
        grid=(slots,),
        in_specs=[
            pl.BlockSpec((1, keys, both), lambda i: (i, 0, 0)),
            pl.BlockSpec((vertices, width), lambda i: (0, 0)),
        ],
        out_specs=pl.BlockSpec((1, width, vertices), lambda i: (i, 0, 0)),
        out_shape=jax.ShapeDtypeStruct((slots, width, vertices), jnp.bfloat16),
        compiler_params=pltpu.CompilerParams(vmem_limit_bytes=32 * MIB),
        name="decoder",
    )(slot_pairs, queries)


def solution(mesh):
    placed = (
        P("frame", None, None),
        P("frame", None, None, "mp"),
        P("mp", None),
        P(),
        P(None, None, "mp"),
        P("mp", None),
        P(),
        P(None, None, "mp"),
        P(None, "mp"),
        P(),
        P(),
        P(),
    )
    return jax.shard_map(
        on_device_pair if mesh.shape["mp"] == 2 else on_device_any,
        mesh=mesh,
        in_specs=placed,
        out_specs=(P("frame", "mp", None), P("frame", None, "mp")),
        check_vma=False,
    )
```

```python
import functools

import jax
import jax.numpy as jnp
from jax import lax
from jax.experimental import pallas as pl
from jax.experimental.pallas import tpu as pltpu
from jax.sharding import PartitionSpec as P

HD = 80
TILE = 128
MAXC = 3
RCAP = 4
DEC_HD = 64
V = 778
ROWS = 256
PATCHES = 16
CHUNKS = 2
LOG2E = 1.4426950408889634
MIB = 1 << 20


def layer_norm(values, gain_row):
    row_mean = jnp.mean(values, axis=-1, keepdims=True)
    centred = values - row_mean
    spread = jnp.mean(centred * centred, axis=-1, keepdims=True)
    return (centred * lax.rsqrt(spread + 1e-06) * gain_row.astype(jnp.float32)).astype(jnp.bfloat16)


def soft_weights(scores):
    row_top = jnp.max(scores, axis=-1, keepdims=True)
    raised = jnp.exp(scores - row_top)
    return (raised / jnp.sum(raised, axis=-1, keepdims=True)).astype(jnp.bfloat16)


def crop_slots(crop_counts, crop_owner):
    frames_all, most = crop_owner.shape
    live_slots = (jnp.arange(most, dtype=jnp.int32)[None, :] < crop_counts[:, None]).reshape(-1)
    owner_flat = crop_owner.reshape(-1)
    owner_hits = (
        (owner_flat[:, None] == jnp.arange(frames_all, dtype=jnp.int32)[None, :])
        & live_slots[:, None]
    ).astype(jnp.int32)
    before = jnp.cumsum(owner_hits, axis=0) - owner_hits
    slot_rank = jnp.sum(before * owner_hits, axis=1)
    return (live_slots, owner_flat * RCAP + slot_rank)


def on_device_any(
    stream,
    spatial_qkv,
    spatial_out_w,
    temporal_gain,
    temporal_qkv_w,
    temporal_out_w,
    decoder_gain,
    decoder_kv_w,
    vertex_queries,
    crop_counts,
    crop_tiles,
    crop_owner,
):
    patches = stream.shape[1]
    model_width = stream.shape[2]
    local_cols = spatial_qkv.shape[3]
    heads_here = local_cols // HD
    score_scale = HD ** (-0.5)
    spatial_query = spatial_qkv[0, :, 0].reshape(patches, heads_here, HD)
    spatial_key = spatial_qkv[0, :, 1].reshape(patches, heads_here, HD)
    spatial_value = spatial_qkv[0, :, 2].reshape(patches, heads_here, HD)
    scores = (
        jnp.einsum("qhd,khd->hqk", spatial_query, spatial_key, preferred_element_type=jnp.float32)
        * score_scale
    )
    weights = soft_weights(scores)
    spatial_heads = (
        jnp.einsum("hqk,khd->qhd", weights, spatial_value, preferred_element_type=jnp.float32)
        .astype(jnp.bfloat16)
        .reshape(patches, local_cols)
    )
    spatial_part = jnp.dot(spatial_heads, spatial_out_w, preferred_element_type=jnp.float32)
    spatial_total = lax.psum(spatial_part.astype(jnp.bfloat16), "mp").astype(jnp.float32)
    middle = (stream[0].astype(jnp.float32) + spatial_total).astype(jnp.bfloat16)
    normed = layer_norm(middle.astype(jnp.float32), temporal_gain)
    projected = jnp.stack(
        [
            jnp.dot(normed, temporal_qkv_w[which], preferred_element_type=jnp.float32).astype(
                jnp.bfloat16
            )
            for which in range(3)
        ],
        axis=1,
    )[None]
    gathered = lax.all_to_all(projected, "frame", split_axis=1, concat_axis=0, tiled=True)
    frames_all = gathered.shape[0]
    patch_rows = gathered.shape[1]
    temporal_query = gathered[:, :, 0].reshape(frames_all, patch_rows, heads_here, HD)
    temporal_key = gathered[:, :, 1].reshape(frames_all, patch_rows, heads_here, HD)
    temporal_value = gathered[:, :, 2].reshape(frames_all, patch_rows, heads_here, HD)
    frame_scores = (
        jnp.einsum(
            "fphd,gphd->phfg", temporal_query, temporal_key, preferred_element_type=jnp.float32
        )
        * score_scale
    )
    frame_weights = soft_weights(frame_scores)
    mixed_heads = (
        jnp.einsum(
            "phfg,gphd->fphd", frame_weights, temporal_value, preferred_element_type=jnp.float32
        )
        .astype(jnp.bfloat16)
        .reshape(frames_all, patch_rows, local_cols)
    )
    frame_heads = lax.all_to_all(mixed_heads, "frame", split_axis=0, concat_axis=1, tiled=True)
    temporal_part = jnp.dot(frame_heads[0], temporal_out_w, preferred_element_type=jnp.float32)
    temporal_total = lax.psum(temporal_part.astype(jnp.bfloat16), "mp").astype(jnp.float32)
    final_stream = (middle.astype(jnp.float32) + temporal_total).astype(jnp.bfloat16)
    out_cols = model_width // lax.axis_size("mp")
    stream_part = lax.dynamic_slice_in_dim(
        final_stream, lax.axis_index("mp") * out_cols, out_cols, 1
    )[None]
    frame_id = lax.axis_index("frame")
    my_tiles = lax.dynamic_index_in_dim(crop_tiles, frame_id, 0, keepdims=False)
    tile_view = final_stream.reshape(patches // TILE, TILE, model_width)
    crop_rows = jnp.take(tile_view, my_tiles, axis=0)
    crop_norm = layer_norm(crop_rows.astype(jnp.float32), decoder_gain).reshape(
        MAXC * TILE, model_width
    )
    return decode(
        [crop_norm], lambda part: part, decoder_kv_w, vertex_queries, crop_counts, crop_owner
    ), stream_part


def head_window(head, size):
    first = head * size // 128 * 128
    last = -(-(head + 1) * size // 128) * 128
    return first, last - first, head * size - first


def head_attention(query, key_of, value_of, out_ref, row_slice, heads_here, keep, size=HD):
    factor = size ** (-0.5) * LOG2E
    done = {}
    for head in range(heads_here):
        first, width, start = head_window(head, size)
        lane = lax.broadcasted_iota(jnp.int32, (1, width), 1)
        inside = (lane >= start) & (lane < start + size)
        q_here = query[:, first : first + width]
        q_here = jnp.where(inside, q_here, jnp.zeros_like(q_here))
        scores = lax.dot_general(
            q_here,
            key_of(first, width),
            (((1,), (1,)), ((), ())),
            preferred_element_type=jnp.float32,
        )
        if keep is not None:
            scores = jnp.where(keep, scores, -jnp.inf)
        top = jnp.max(scores, axis=-1, keepdims=True)
        raised = jnp.exp2(scores * factor - top * factor).astype(jnp.bfloat16)
        v_here = value_of(first, width)
        v_here = jnp.where(inside, v_here, jnp.ones_like(v_here))
        both = jnp.dot(raised, v_here, preferred_element_type=jnp.float32)
        at = 0 if start else width - 1
        found = (both / both[:, at : at + 1]).astype(jnp.bfloat16)
        for tile in range(width // 128):
            column = first + tile * 128
            part = found[:, tile * 128 : tile * 128 + 128]
            if column in done:
                part = jnp.where(inside[:, tile * 128 : tile * 128 + 128], part, done[column])
            done[column] = part
    for column, part in done.items():
        out_ref[row_slice, column : column + 128] = part


def spatial_kernel(q_ref, k_ref, v_ref, w_ref, mine_ref, other_ref, heads_ref):
    here = lax.axis_index("mp")
    cols = q_ref.shape[1]
    head_attention(
        q_ref[...],
        lambda first, width: k_ref[:, first : first + width],
        lambda first, width: v_ref[:, first : first + width],
        heads_ref,
        slice(None),
        cols // HD,
        None,
    )
    half = mine_ref.shape[1]
    for out_ref, group in ((mine_ref, here), (other_ref, 1 - here)):
        columns = pl.ds(pl.multiple_of(group * half, 128), half)
        out_ref[...] = jnp.dot(
            heads_ref[...], w_ref[:, columns], preferred_element_type=jnp.float32
        ).astype(jnp.bfloat16)


def spatial_attention(query, key, value, weight):
    patches, cols = query.shape
    half = weight.shape[1] // 2
    whole = lambda i: (0, 0)
    block = lambda i: (i, 0)
    return pl.pallas_call(
        spatial_kernel,
        grid=(patches // ROWS,),
        in_specs=[
            pl.BlockSpec((ROWS, cols), block),
            pl.BlockSpec(key.shape, whole),
            pl.BlockSpec(key.shape, whole),
            pl.BlockSpec(weight.shape, whole),
        ],
        out_specs=[pl.BlockSpec((ROWS, half), block)] * 2,
        out_shape=[jax.ShapeDtypeStruct((patches, half), jnp.bfloat16)] * 2,
        scratch_shapes=[pltpu.VMEM((ROWS, cols), jnp.bfloat16)],
        compiler_params=pltpu.CompilerParams(vmem_limit_bytes=48 * MIB),
        name="spatial",
    )(query, key, value, weight)


def temporal_kernel(
    mid_mine, mid_other, gain_ref, w_ref, out_w_ref, mine_ref, other_ref, qkv_ref, heads_ref
):
    here = lax.axis_index("mp")
    frames_all, rows, half = mid_mine.shape
    total = frames_all * rows
    model = 2 * half
    pair = [
        (ref[...].reshape(total, half).astype(jnp.float32), pl.multiple_of(group * half, 128))
        for ref, group in ((mid_mine, here), (mid_other, 1 - here))
    ]
    mean = sum(jnp.sum(part, axis=-1, keepdims=True) for part, _ in pair) / model
    pair = [(part - mean, first) for part, first in pair]
    spread = sum(jnp.sum(part * part, axis=-1, keepdims=True) for part, _ in pair) / model
    scale = lax.rsqrt(spread + 1e-06)
    pair = [
        (
            (part * scale * gain_ref[:, pl.ds(first, half)].astype(jnp.float32)).astype(
                jnp.bfloat16
            ),
            first,
        )
        for part, first in pair
    ]
    for which in range(3):
        qkv_ref[which] = sum(
            jnp.dot(part, w_ref[which, pl.ds(first, half), :], preferred_element_type=jnp.float32)
            for part, first in pair
        ).astype(jnp.bfloat16)
    row_patch = lax.broadcasted_iota(jnp.int32, (total, total), 0) % rows
    col_patch = lax.broadcasted_iota(jnp.int32, (total, total), 1) % rows
    cols = qkv_ref.shape[2]
    head_attention(
        qkv_ref[0],
        lambda first, width: qkv_ref[1, :, first : first + width],
        lambda first, width: qkv_ref[2, :, first : first + width],
        heads_ref,
        slice(None),
        cols // HD,
        row_patch == col_patch,
    )
    for out_ref, group in ((mine_ref, here), (other_ref, 1 - here)):
        columns = pl.ds(pl.multiple_of(group * half, 128), half)
        out_ref[...] = (
            jnp.dot(heads_ref[...], out_w_ref[:, columns], preferred_element_type=jnp.float32)
            .astype(jnp.bfloat16)
            .reshape(frames_all, rows, half)
        )


def temporal_attention(mid_mine, mid_other, gain, weights, out_weight):
    frames_all, patch_rows, half = mid_mine.shape
    cols = weights.shape[2]
    total = frames_all * PATCHES
    block = pl.BlockSpec((frames_all, PATCHES, half), lambda i: (0, i, 0))
    return pl.pallas_call(
        temporal_kernel,
        grid=(patch_rows // PATCHES,),
        in_specs=[
            block,
            block,
            pl.BlockSpec((1, 2 * half), lambda i: (0, 0)),
            pl.BlockSpec(weights.shape, lambda i: (0, 0, 0)),
            pl.BlockSpec(out_weight.shape, lambda i: (0, 0)),
        ],
        out_specs=[block, block],
        out_shape=[jax.ShapeDtypeStruct(mid_mine.shape, jnp.bfloat16)] * 2,
        scratch_shapes=[
            pltpu.VMEM((3, total, cols), jnp.bfloat16),
            pltpu.VMEM((total, cols), jnp.bfloat16),
        ],
        compiler_params=pltpu.CompilerParams(vmem_limit_bytes=48 * MIB),
        name="temporal",
    )(mid_mine, mid_other, gain.reshape(1, -1), weights, out_weight)


def swap(values):
    return lax.ppermute(values, "mp", [(0, 1), (1, 0)])


def added(base, mine, other):
    update = mine.astype(jnp.float32) + other.astype(jnp.float32)
    return (base.astype(jnp.float32) + update).astype(jnp.bfloat16)


def on_device_pair(
    stream,
    spatial_qkv,
    spatial_out_w,
    temporal_gain,
    temporal_qkv_w,
    temporal_out_w,
    decoder_gain,
    decoder_kv_w,
    vertex_queries,
    crop_counts,
    crop_tiles,
    crop_owner,
):
    patches = stream.shape[1]
    half = stream.shape[2] // 2
    frames_all = crop_owner.shape[0]
    here = lax.axis_index("mp")
    own_rows = patches // frames_all
    part_rows = own_rows // CHUNKS

    def chunk_of(values, chunk):
        split = values.reshape(frames_all, CHUNKS, part_rows, values.shape[1])
        return split[:, chunk].reshape(frames_all * part_rows, values.shape[1])

    key, value = spatial_qkv[0, :, 1], spatial_qkv[0, :, 2]
    stream_half = lax.dynamic_slice_in_dim(stream[0], here * half, half, 1)
    arrived = []
    for chunk in range(CHUNKS):
        mine, theirs = spatial_attention(
            chunk_of(spatial_qkv[0, :, 0], chunk), key, value, spatial_out_w
        )
        middle = added(chunk_of(stream_half, chunk), mine, swap(theirs))
        arrived.append(
            lax.all_to_all(
                middle.reshape(frames_all, part_rows, half),
                "frame",
                split_axis=0,
                concat_axis=0,
                tiled=True,
            )
        )
    returned = []
    for mid_mine in arrived:
        mine, theirs = temporal_attention(
            mid_mine, swap(mid_mine), temporal_gain, temporal_qkv_w, temporal_out_w
        )
        final_mine = added(mid_mine, mine, swap(theirs))
        returned.append(
            lax.all_to_all(final_mine, "frame", split_axis=0, concat_axis=0, tiled=True)
        )
    stream_part = jnp.stack(returned, axis=1).reshape(1, patches, half)
    frame_id = lax.axis_index("frame")
    my_tiles = lax.dynamic_index_in_dim(crop_tiles, frame_id, 0, keepdims=False)

    def crop_norm_of(part):
        tile_view = part.reshape(patches // TILE, TILE // CHUNKS, half)
        crop_mine = jnp.concatenate(
            [
                lax.dynamic_index_in_dim(tile_view, my_tiles[slot], 0, keepdims=False)
                for slot in range(MAXC)
            ],
            axis=0,
        )
        crop_other = swap(crop_mine)
        crop_rows = jnp.where(
            here == 0,
            jnp.concatenate([crop_mine, crop_other], axis=1),
            jnp.concatenate([crop_other, crop_mine], axis=1),
        )
        return layer_norm(crop_rows.astype(jnp.float32), decoder_gain)

    return decode(returned, crop_norm_of, decoder_kv_w, vertex_queries, crop_counts, crop_owner), stream_part


def decode(parts, crop_norm_of, decoder_kv_w, vertex_queries, crop_counts, crop_owner):
    frame_id = lax.axis_index("frame")
    frames_all = crop_owner.shape[0]
    dec_local = decoder_kv_w.shape[2]
    live_slots, slot_index = crop_slots(crop_counts, crop_owner)
    targets = frame_id * RCAP + jnp.arange(RCAP, dtype=jnp.int32)
    choose = ((slot_index[None, :] == targets[:, None]) & live_slots[None, :]).astype(jnp.float32)
    my_owner = lax.dynamic_index_in_dim(crop_owner, frame_id, 0, keepdims=False)
    my_count = lax.dynamic_index_in_dim(crop_counts, frame_id, 0, keepdims=False)
    my_live = jnp.arange(MAXC, dtype=jnp.int32) < my_count
    to_owner = (
        (my_owner[None, :] == jnp.arange(frames_all, dtype=jnp.int32)[:, None]) & my_live[None, :]
    ).astype(jnp.bfloat16)
    by_frame = choose.reshape(RCAP, frames_all, MAXC).sum(axis=2).astype(jnp.bfloat16)
    pieces = []
    outgoing = None
    for part in parts:
        if outgoing is not None:
            part, outgoing = lax.optimization_barrier((part, outgoing))
            pieces.append(outgoing)
        crop_norm = crop_norm_of(part)
        crop_keys = jnp.dot(crop_norm, decoder_kv_w[0], preferred_element_type=jnp.float32).astype(
            jnp.bfloat16
        )
        crop_values = jnp.dot(crop_norm, decoder_kv_w[1], preferred_element_type=jnp.float32).astype(
            jnp.bfloat16
        )
        crop_pairs = jnp.concatenate([crop_keys, crop_values], axis=1).reshape(
            MAXC, -1, 2 * dec_local
        )
        outgoing = jnp.einsum(
            "nm,mtc->ntc", to_owner, crop_pairs, preferred_element_type=jnp.float32
        ).astype(jnp.bfloat16)
    pieces.append(outgoing)
    for index, outgoing in enumerate(pieces):
        incoming = lax.all_to_all(outgoing, "frame", split_axis=0, concat_axis=0, tiled=True)
        piece = jnp.einsum(
            "rg,gtc->rtc", by_frame, incoming, preferred_element_type=jnp.float32
        ).astype(jnp.bfloat16)
        pieces[index] = piece
    slot_pairs = jnp.concatenate(pieces, axis=1)
    if dec_local % 128 == 0:
        return vertex_decoder(slot_pairs, vertex_queries)
    heads_dec = dec_local // DEC_HD
    slot_keys = slot_pairs[:, :, :dec_local].reshape(RCAP, TILE, heads_dec, DEC_HD)
    slot_values = slot_pairs[:, :, dec_local:].reshape(RCAP, TILE, heads_dec, DEC_HD)
    queries = vertex_queries.reshape(V, heads_dec, DEC_HD)
    vertex_scores = jnp.einsum(
        "vhd,rthd->rhvt", queries, slot_keys, preferred_element_type=jnp.float32
    ) * DEC_HD ** (-0.5)
    vertex_weights = soft_weights(vertex_scores)
    decoded = jnp.einsum(
        "rhvt,rthd->rhdv", vertex_weights, slot_values, preferred_element_type=jnp.float32
    )
    return decoded.astype(jnp.bfloat16).reshape(RCAP, dec_local, V)


def decoder_kernel(pair_ref, query_ref, out_ref):
    cols = query_ref.shape[1]
    head_attention(
        query_ref[...],
        lambda first, width: pair_ref[0, :, first : first + width],
        lambda first, width: pair_ref[0, :, cols + first : cols + first + width],
        out_ref.at[0],
        slice(None),
        cols // DEC_HD,
        None,
        DEC_HD,
    )


def vertex_decoder(slot_pairs, queries):
    slots, keys, both = slot_pairs.shape
    vertices, width = queries.shape
    return pl.pallas_call(
        decoder_kernel,
        grid=(slots,),
        in_specs=[
            pl.BlockSpec((1, keys, both), lambda i: (i, 0, 0)),
            pl.BlockSpec((vertices, width), lambda i: (0, 0)),
        ],
        out_specs=pl.BlockSpec((1, vertices, width), lambda i: (i, 0, 0)),
        out_shape=jax.ShapeDtypeStruct((slots, vertices, width), jnp.bfloat16),
        compiler_params=pltpu.CompilerParams(vmem_limit_bytes=32 * MIB),
        name="decoder",
    )(slot_pairs, queries).transpose(0, 2, 1)


def solution(mesh):
    placed = (
        P("frame", None, None),
        P("frame", None, None, "mp"),
        P("mp", None),
        P(),
        P(None, None, "mp"),
        P("mp", None),
        P(),
        P(None, None, "mp"),
        P(None, "mp"),
        P(),
        P(),
        P(),
    )
    return jax.shard_map(
        on_device_pair if mesh.shape["mp"] == 2 else on_device_any,
        mesh=mesh,
        in_specs=placed,
        out_specs=(P("frame", "mp", None), P("frame", None, "mp")),
        check_vma=False,
    )
```
